32 devices in a mesh: ctx: 16 (over z, y, x), kvh: 2 (over core).
Axes of the slice: x: 2, y: 2, z: 4, core: 2. Of those that a mesh axis runs over, the one named last changes fastest.
Arguments:
- doc_lengths: int32 [9], replicated, may hold values from 1 to 896, 4096 in all
- queries: bfloat16 [4096, 1024], P('ctx', 'kvh'), may hold values from -6 to 6
- keys: bfloat16 [4096, 256], P('ctx', 'kvh'), may hold values from -6 to 6
- values: bfloat16 [4096, 256], P('ctx', 'kvh'), may hold values from -12 to 12
- o_weight: bfloat16 [1024, 4096], P('kvh'), may hold values from -0.1875 to 0.1875
Outputs:
- projected: bfloat16 [4096, 4096], P(('ctx', 'kvh'))
The draws below stay inside these ranges and needn't reach their ends.
Inputs may be any that keep to these rules, and one draw needn't show every extreme that they name: `doc_lengths`: the documents in sequence order; they sum to 4096.
All inputs are finite; a program needn't handle non-finite values.
Results may differ from the reference program's by a relative error of at most 0.018.
Values may be sent and summed in bfloat16 or wider, within the bound.
A program may use at most 64 MiB of HBM per device.

```python
import math
import jax
import jax.numpy as jnp
import numpy as np
from jax import lax

D = 4096
HEAD_WIDTH = 128
QUERY_PER_KEY = 4
KEY_HEADS = 2
HQ = 8
TOK_DEV = 256
STRETCH = 128
PACKED_LENGTH = 4096
DOCUMENT_LIMIT = 896
NDOCS = 9
N_KVH = 2


def draw_queries(key, part):
    sampled_tensors = jax.random.truncated_normal(jax.random.fold_in(key, 11), -6.0, 6.0, (PACKED_LENGTH, KEY_HEADS, QUERY_PER_KEY, HEAD_WIDTH), jnp.float32)
    return sampled_tensors.reshape(PACKED_LENGTH, HQ * HEAD_WIDTH).astype(jnp.bfloat16)


def draw_keys(key, part):
    sampled_tensors = jax.random.truncated_normal(jax.random.fold_in(key, 12), -6.0, 6.0, (PACKED_LENGTH, KEY_HEADS, HEAD_WIDTH), jnp.float32)
    return sampled_tensors.reshape(PACKED_LENGTH, KEY_HEADS * HEAD_WIDTH).astype(jnp.bfloat16)


def draw_values(key, part):
    sampled_tensors = jax.random.truncated_normal(jax.random.fold_in(key, 13), -4.0, 4.0, (PACKED_LENGTH, KEY_HEADS * HEAD_WIDTH), jnp.float32)
    row_scale = jnp.exp(jax.random.uniform(jax.random.fold_in(key, 14), (PACKED_LENGTH,), jnp.float32, math.log(0.3), math.log(3.0)))
    return (sampled_tensors * row_scale[:, None]).astype(jnp.bfloat16)


def shard_levels(stream_key, shape, shards, smallest, top_value):
    gain, own = 1.0, jax.random.fold_in(stream_key, 6)
    for dim, parts in shards:
        heights = jnp.exp(jax.random.uniform(jax.random.fold_in(own, dim), (parts,), jnp.float32, smallest / len(shards), top_value / len(shards)))
        gain = gain * jnp.repeat(heights, shape[dim] // parts).reshape([-1 if axis == dim else 1 for axis in range(len(shape))])
    return gain


def profile(number_of, total, bound, skew):
    weights = [(1 << 20) // math.isqrt(grade ** skew) + 1 for grade in range(2, number_of + 1)]
    surplus, holding = total - bound - (number_of - 1), [1] * (number_of - 1)
    while surplus > 0:
        candidates = [i for i in range(number_of - 1) if holding[i] < bound]
        pool, left = sum([weights[i] for i in candidates]), surplus
        for i in candidates:
            more = min(bound - holding[i], max(1, left * weights[i] // pool), surplus)
            holding[i] = holding[i] + more
            surplus = surplus - more
    return np.array([bound] + holding)


def ragged(rng, number_of, total, bound, skew):
    if number_of == 2:
        one = jax.random.randint(rng, (), max(1, total - bound), min(bound, total - 1) + 1)
        return jnp.stack([one, total - one])
    sizes = jnp.asarray(profile(number_of, total, bound, skew), jnp.int32)
    twos = (number_of - 1) // 2
    giver, taker = sizes[1:1 + 2 * twos:2], sizes[2:2 + 2 * twos:2]
    slack = jnp.minimum(giver - 1, bound - taker)
    shifted = jax.random.randint(jax.random.fold_in(rng, 1), (twos,), 0, 1 << 20) % (slack + 1)
    sizes = sizes.at[1:1 + 2 * twos:2].set(giver - shifted).at[2:2 + 2 * twos:2].set(taker + shifted)
    return sizes[jax.random.permutation(jax.random.fold_in(rng, 2), number_of)]


def normal_values(key, shape, deviation, reach, shards=(), held_as=jnp.bfloat16):
    level = shard_levels(key, shape, shards, -0.22, 0.18) if shards else 1.0
    array = jax.random.normal(key, shape, jnp.float32) * deviation * level
    return jnp.minimum(jnp.maximum(array, -reach), reach).astype(held_as)


def setup_inputs(seed: int = 0) -> dict:
    key_list = jax.random.split(jax.random.key(seed), 6)
    doc_lengths = ragged(key_list[0], NDOCS, PACKED_LENGTH, DOCUMENT_LIMIT, 1).astype(jnp.int32)
    queries = draw_queries(jax.random.fold_in(key_list[5], 71), 0)
    keys = draw_keys(jax.random.fold_in(key_list[5], 71), 0)
    values = draw_values(jax.random.fold_in(key_list[5], 71), 0)
    o_weight = normal_values(key_list[4], (HQ * HEAD_WIDTH, D), (HQ * HEAD_WIDTH) ** -0.5, 0.1875, ((0, 2),))
    return {"doc_lengths": doc_lengths, "queries": queries, "keys": keys, "values": values, "o_weight": o_weight}


NEG_FILL = -1e+30

def reference(doc_lengths, queries, keys, values, o_weight):
    row_ids = jnp.arange(PACKED_LENGTH, dtype=jnp.int32)
    source_index = row_ids // TOK_DEV
    offset_rows = row_ids % TOK_DEV
    places = jnp.where(offset_rows < STRETCH, source_index * STRETCH + offset_rows, PACKED_LENGTH - (source_index + 2) * STRETCH + offset_rows).astype(jnp.int32)
    plain_layout = jnp.zeros((PACKED_LENGTH,), jnp.int32).at[places].set(row_ids)
    doc_ends = jnp.cumsum(doc_lengths).astype(jnp.int32)
    documents = lax.optimization_barrier(jnp.sum((doc_ends[None, :] <= row_ids[:, None]).astype(jnp.int32), axis=1)).astype(jnp.int32)
    query_plain = queries[plain_layout].reshape(PACKED_LENGTH, KEY_HEADS, QUERY_PER_KEY, HEAD_WIDTH)
    key_plain = keys[plain_layout].reshape(PACKED_LENGTH, KEY_HEADS, HEAD_WIDTH)
    value_plain = values[plain_layout].reshape(PACKED_LENGTH, KEY_HEADS, HEAD_WIDTH)
    key_padded = jnp.concatenate([jnp.zeros((DOCUMENT_LIMIT, KEY_HEADS, HEAD_WIDTH), key_plain.dtype), key_plain], axis=0)
    value_padded = jnp.concatenate([jnp.zeros((DOCUMENT_LIMIT, KEY_HEADS, HEAD_WIDTH), value_plain.dtype), value_plain], axis=0)
    doc_pad = jnp.concatenate([jnp.full((DOCUMENT_LIMIT,), -1, jnp.int32), documents], axis=0)
    scaling = 1.0 / math.sqrt(HEAD_WIDTH)

    def one_block(block_index):
        first_row = (block_index * STRETCH).astype(jnp.int32)
        query_part = lax.dynamic_slice_in_dim(query_plain, first_row, STRETCH, 0).astype(jnp.float32)
        key_part = lax.dynamic_slice_in_dim(key_padded, first_row, STRETCH + DOCUMENT_LIMIT, 0).astype(jnp.float32)
        value_part = lax.dynamic_slice_in_dim(value_padded, first_row, STRETCH + DOCUMENT_LIMIT, 0).astype(jnp.float32)
        key_docs = lax.dynamic_slice_in_dim(doc_pad, first_row, STRETCH + DOCUMENT_LIMIT, 0)
        query_docs = lax.dynamic_slice_in_dim(documents, first_row, STRETCH, 0)
        query_places = first_row + jnp.arange(STRETCH, dtype=jnp.int32)
        key_places = first_row - DOCUMENT_LIMIT + jnp.arange(STRETCH + DOCUMENT_LIMIT, dtype=jnp.int32)
        allowed = (key_docs[None, :] == query_docs[:, None]) & (key_places[None, :] <= query_places[:, None])
        scores = jnp.einsum('cgjd,kgd->cgjk', query_part, key_part) * scaling
        scores = jnp.where(allowed[:, None, None, :], scores, NEG_FILL)
        highest = lax.optimization_barrier(jnp.max(scores, axis=3, keepdims=True))
        weights = jnp.where(allowed[:, None, None, :], jnp.exp(scores - highest), 0.0)
        weights = weights / lax.optimization_barrier(jnp.sum(weights, axis=3, keepdims=True))
        weights = lax.optimization_barrier(weights.astype(jnp.bfloat16)).astype(jnp.float32)
        result = jnp.einsum('cgjk,kgd->cgjd', weights, value_part)
        return result.reshape(STRETCH, HQ * HEAD_WIDTH).astype(jnp.bfloat16)
    blocks_nat = lax.map(one_block, jnp.arange(PACKED_LENGTH // STRETCH, dtype=jnp.int32)).reshape(PACKED_LENGTH, HQ * HEAD_WIDTH)
    attention = blocks_nat[places]
    grouped = attention.reshape(PACKED_LENGTH, N_KVH, HQ * HEAD_WIDTH // N_KVH)
    weight_groups = o_weight.reshape(N_KVH, HQ * HEAD_WIDTH // N_KVH, D)
    summed = jnp.zeros((PACKED_LENGTH, D), jnp.float32)
    for group in range(N_KVH):
        partial_value = jnp.dot(grouped[:, group], weight_groups[group], preferred_element_type=jnp.float32).astype(jnp.bfloat16)
        partial_value = lax.optimization_barrier(partial_value)
        summed = summed + partial_value.astype(jnp.float32)
    return summed.astype(jnp.bfloat16)
```

```python
import functools
import math

import jax
import jax.numpy as jnp
from jax import lax
from jax.experimental import pallas as pl
from jax.experimental.pallas import tpu as pltpu
from jax.sharding import PartitionSpec as P

HEAD_WIDTH = 128
REACH = 7
CHUNK = 4
TILE = 512
NEG_FILL = -1e30


def kernel(
    n_ctx, n_kvh, docs, q_hbm, k_hbm, v_hbm, w_hbm, o_ref,
    kv, q, w, att, sbuf, rbuf,
    local_sem, send_a, send_b, recv, rs_send, rs_recv,
):
    i = lax.axis_index("ctx")
    g = lax.axis_index("kvh")
    rows = q.shape[0]
    half = rows // 2
    heads = q.shape[1] // HEAD_WIDTH
    span = REACH + 1
    last = 2 * n_ctx - 1
    out_rows = rows // n_kvh
    tiles = w.shape[1] // TILE
    own_gap = last - 2 * i

    def own_copies():
        for x in range(2):
            for j, ref in enumerate((k_hbm, v_hbm)):
                yield pltpu.make_async_copy(
                    ref.at[pl.ds(x * half, half)], kv.at[x * span, j], local_sem.at[2 * x + j]
                )

    own = list(own_copies())
    for copy in own:
        copy.start()

    barrier = pltpu.get_barrier_semaphore()

    def greet(chip):
        pl.semaphore_signal(
            barrier, inc=1, device_id={"ctx": chip}, device_id_type=pl.DeviceIdType.MESH
        )

    for d in range(1, REACH + 1):

        @pl.when(i >= d)
        def _():
            greet(i - d)

        @pl.when(i + d < n_ctx)
        def _():
            greet(i + d)

        @pl.when((i + d >= n_ctx) & (own_gap != d))
        def _():
            greet(last - i - d)

    for j in range(1, n_kvh):
        pl.semaphore_signal(
            barrier,
            inc=1,
            device_id={"kvh": lax.rem(g + j, n_kvh)},
            device_id_type=pl.DeviceIdType.MESH,
        )

    q_copy = pltpu.make_async_copy(q_hbm, q, local_sem.at[4])
    w_copy = pltpu.make_async_copy(w_hbm, w, local_sem.at[5])
    q_copy.start()
    for d in range(1, REACH + 1):

        @pl.when(i < d)
        def _():
            kv[d] = jnp.zeros(kv.shape[1:], kv.dtype)

    for copy in own:
        copy.wait()
    for d in range(1, REACH + 1):

        @pl.when(own_gap == d)
        def _():
            kv[span + d] = kv[0]

    selfs = jnp.where(own_gap <= REACH, 1, 0)
    pl.semaphore_wait(barrier, REACH - selfs + jnp.minimum(i, REACH) + n_kvh - 1)

    def send(x, slot, chip, sem):
        return pltpu.make_async_remote_copy(
            src_ref=kv.at[x * span],
            dst_ref=kv.at[slot],
            send_sem=sem,
            recv_sem=recv.at[slot],
            device_id={"ctx": chip},
            device_id_type=pl.DeviceIdType.MESH,
        )

    def each_send(act):
        for d in range(1, REACH + 1):

            @pl.when(i + d < n_ctx)
            def _():
                act(send(0, d, i + d, send_a.at[d]))

            @pl.when((i + d >= n_ctx) & (own_gap != d))
            def _():
                act(send(0, span + d, last - i - d, send_a.at[d]))

            @pl.when(i >= d)
            def _():
                act(send(1, span + d, i - d, send_b.at[d]))

    each_send(lambda copy: copy.start())
    w_copy.start()

    scale = math.log2(math.e) / math.sqrt(HEAD_WIDTH)
    q_copy.wait()

    def attend(x):
        stretch = x * last + (1 - 2 * x) * i
        base = pl.multiple_of(x * half, half)
        here = stretch * half + lax.broadcasted_iota(jnp.int32, (half, 1), 0)
        start = jnp.zeros((half, 1), jnp.int32)
        end = jnp.int32(0)
        for n in range(docs.shape[0]):
            end = end + docs[n]
            start = jnp.maximum(start, jnp.where(end <= here, end, 0))
        state = [None] * heads
        for first in range(0, span, CHUNK):
            for d in range(max(first, 1), first + CHUNK):

                @pl.when(((x == 0) & (i >= d)) | ((x == 1) & (own_gap != d)))
                def _():
                    slot = x * span + d
                    pltpu.make_async_copy(kv.at[slot], kv.at[slot], recv.at[slot]).wait()

            part = kv[pl.ds(x * span + first, CHUNK)]
            k = part[:, 0].reshape(CHUNK * half, HEAD_WIDTH)
            v = part[:, 1].reshape(CHUNK * half, HEAD_WIDTH)
            column = lax.broadcasted_iota(jnp.int32, (half, CHUNK * half), 1)
            there = (stretch - first) * half + column - 2 * half * (column // half)
            bias = jnp.where((there >= start) & (there <= here), 0.0, NEG_FILL)
            for h in range(heads):
                lanes = slice(h * HEAD_WIDTH, (h + 1) * HEAD_WIDTH)
                score = (
                    lax.dot_general(
                        q[pl.ds(base, half), lanes],
                        k,
                        (((1,), (1,)), ((), ())),
                        preferred_element_type=jnp.float32,
                    )
                    + bias
                )
                top = jnp.max(score, axis=1, keepdims=True)
                if first:
                    top = jnp.maximum(top, state[h][0])
                weight = jnp.exp2((score - top) * scale)
                total = jnp.sum(weight, axis=1, keepdims=True)
                out = jnp.dot(weight.astype(jnp.bfloat16), v, preferred_element_type=jnp.float32)
                if first:
                    factor = jnp.exp2((state[h][0] - top) * scale)
                    total = total + state[h][1] * factor
                    out = out + state[h][2] * factor
                state[h] = (top, total, out)
        for h in range(heads):
            lanes = slice(h * HEAD_WIDTH, (h + 1) * HEAD_WIDTH)
            att[pl.ds(base, half), lanes] = (state[h][2] / state[h][1]).astype(att.dtype)

    def project(p, t):
        return jnp.dot(
            att[pl.ds(pl.multiple_of(p * out_rows, out_rows), out_rows), :],
            w[:, t * TILE : (t + 1) * TILE],
            preferred_element_type=jnp.float32,
        )

    def hand_over(j, t):
        return pltpu.make_async_remote_copy(
            src_ref=sbuf.at[j - 1, t],
            dst_ref=rbuf.at[j - 1, t],
            send_sem=rs_send.at[j - 1, t],
            recv_sem=rs_recv.at[j - 1, t],
            device_id={"kvh": lax.rem(g + j, n_kvh)},
            device_id_type=pl.DeviceIdType.MESH,
        )

    def give():
        for j in range(1, n_kvh):
            for t in range(tiles):
                sbuf[j - 1, t] = project(lax.rem(g + j, n_kvh), t).astype(sbuf.dtype)
                hand_over(j, t).start()

    if n_kvh == 2:
        attend(1 - g)
        w_copy.wait()
        give()
        attend(g)
    else:
        attend(0)
        attend(1)
        w_copy.wait()
        give()
    for t in range(tiles):
        total = project(g, t)
        for j in range(1, n_kvh):
            hand_over(j, t).wait_recv()
            total = total + rbuf[j - 1, t].astype(jnp.float32)
        o_ref[:, t * TILE : (t + 1) * TILE] = total.astype(o_ref.dtype)
    each_send(lambda copy: copy.wait_send())
    for j in range(1, n_kvh):
        for t in range(tiles):
            hand_over(j, t).wait_send()


def local(n_ctx, n_kvh, doc_lengths, queries, keys, values, o_weight):
    rows, width = queries.shape
    half = rows // 2
    columns = o_weight.shape[1]
    out_rows = rows // n_kvh
    tiles = columns // TILE
    span = REACH + 1
    dtype = queries.dtype
    any_spec = pl.BlockSpec(memory_space=pl.ANY)
    return pl.pallas_call(
        functools.partial(kernel, n_ctx, n_kvh),
        out_shape=jax.ShapeDtypeStruct((out_rows, columns), dtype),
        in_specs=[pl.BlockSpec(memory_space=pltpu.SMEM)] + [any_spec] * 4,
        out_specs=pl.BlockSpec(memory_space=pltpu.VMEM),
        scratch_shapes=[
            pltpu.VMEM((2 * span, 2, half, HEAD_WIDTH), dtype),
            pltpu.VMEM((rows, width), dtype),
            pltpu.VMEM(o_weight.shape, dtype),
            pltpu.VMEM((rows, width), dtype),
            pltpu.VMEM((n_kvh - 1, tiles, out_rows, TILE), dtype),
            pltpu.VMEM((n_kvh - 1, tiles, out_rows, TILE), dtype),
            pltpu.SemaphoreType.DMA((6,)),
            pltpu.SemaphoreType.DMA((span,)),
            pltpu.SemaphoreType.DMA((span,)),
            pltpu.SemaphoreType.DMA((2 * span,)),
            pltpu.SemaphoreType.DMA((n_kvh - 1, tiles)),
            pltpu.SemaphoreType.DMA((n_kvh - 1, tiles)),
        ],
        compiler_params=pltpu.CompilerParams(
            collective_id=0, has_side_effects=True, vmem_limit_bytes=60 * 2**20
        ),
    )(doc_lengths, queries, keys, values, o_weight)


def solution(mesh):
    in_specs = (P(), P("ctx", "kvh"), P("ctx", "kvh"), P("ctx", "kvh"), P("kvh", None))
    out_specs = P(("ctx", "kvh"), None)
    return jax.shard_map(
        functools.partial(local, mesh.shape["ctx"], mesh.shape["kvh"]),
        mesh=mesh,
        in_specs=in_specs,
        out_specs=out_specs,
        check_vma=False,
    )
```

```python
import functools
import math

import jax
import jax.numpy as jnp
from jax import lax
from jax.experimental import pallas as pl
from jax.experimental.pallas import tpu as pltpu
from jax.sharding import PartitionSpec as P

HEAD_WIDTH = 128
GROUP = 4
CHUNK = 4
TILE = 512
NEG_FILL = -1e30


def kernel(
    n_ctx, n_kvh, docs, q_hbm, k_hbm, v_hbm, w_hbm, o_ref,
    kv, q, w, att, sbuf, rbuf,
    local_sem, send_sem, recv, rs_send, rs_recv,
):
    i = lax.axis_index("ctx")
    g = lax.axis_index("kvh")
    rows = q.shape[0]
    half = rows // 2
    heads = q.shape[1] // HEAD_WIDTH
    last = 2 * n_ctx - 1
    groups = n_ctx // GROUP
    p = i // GROUP
    b = i % GROUP
    peers = (b + 1 - 2 * (b % 2), (b + 2) % GROUP, 3 - b)
    has_above = p < groups - 1
    has_below = p > 0
    out_rows = rows // n_kvh
    tiles = w.shape[1] // TILE

    def own_copies():
        for x in range(2):
            for j, ref in enumerate((k_hbm, v_hbm)):
                yield pltpu.make_async_copy(
                    ref.at[pl.ds(x * half, half)], kv.at[8 + 4 * x + b, j], local_sem.at[2 * x + j]
                )

    own = list(own_copies())
    for copy in own:
        copy.start()

    barrier = pltpu.get_barrier_semaphore()

    def greet(**device):
        pl.semaphore_signal(
            barrier, inc=1, device_id=device, device_id_type=pl.DeviceIdType.MESH
        )

    @pl.when(has_above)
    def _():
        greet(ctx=i + GROUP)

    @pl.when(has_below)
    def _():
        greet(ctx=i - GROUP)

    for c in peers[:2]:
        greet(ctx=p * GROUP + c)
    for j in range(1, n_kvh):
        greet(kvh=lax.rem(g + j, n_kvh))

    q_copy = pltpu.make_async_copy(q_hbm, q, local_sem.at[4])
    w_copy = pltpu.make_async_copy(w_hbm, w, local_sem.at[5])
    q_copy.start()

    @pl.when(p < 2)
    def _():
        kv[0:4] = jnp.zeros((4, *kv.shape[1:]), kv.dtype)

    @pl.when(p < 1)
    def _():
        kv[4:8] = jnp.zeros((4, *kv.shape[1:]), kv.dtype)

    for copy in own:
        copy.wait()
    ends = jnp.where(has_above, 1, 0) + jnp.where(has_below, 1, 0)
    pl.semaphore_wait(barrier, 2 + ends + n_kvh - 1)

    def send(source, slot, chip, sem):
        return pltpu.make_async_remote_copy(
            src_ref=kv.at[source],
            dst_ref=kv.at[slot],
            send_sem=send_sem.at[sem],
            recv_sem=recv.at[slot],
            device_id={"ctx": chip},
            device_id_type=pl.DeviceIdType.MESH,
        )

    def arrive(slot):
        pltpu.make_async_copy(kv.at[slot], kv.at[slot], recv.at[slot]).wait()

    def up(c, sem, act):
        @pl.when(has_above)
        def _():
            act(send(8 + c, 4 + c, i + GROUP, sem))

    def down(c, sem, act):
        @pl.when(has_below)
        def _():
            act(send(12 + c, 16 + c, i - GROUP, sem))

    def up_again(c, act):
        @pl.when(has_above & has_below & (c > b))
        def _():
            act(send(4 + c, c, i + GROUP, 14 + c))

    def down_again(c, act):
        @pl.when(has_below & (c < b))
        def _():
            act(send(16 + c, 20 + c, i - GROUP, 18 + c))

    def give_own(k, act):
        act(send(8 + b, 8 + b, p * GROUP + peers[k], 2 * k))
        act(send(12 + b, 12 + b, p * GROUP + peers[k], 2 * k + 1))

    def pass_on(act):
        act(send(8 + peers[0], 8 + peers[0], p * GROUP + peers[1], 4))
        act(send(12 + peers[1], 12 + peers[1], p * GROUP + peers[0], 5))

    def start(copy):
        copy.start()

    up(b, 6, start)
    down(b, 7, start)
    give_own(0, start)
    give_own(1, start)
    w_copy.start()
    cx, cy, cd = peers
    arrive(8 + cx)
    up(cx, 8, start)
    arrive(12 + cy)
    pass_on(start)
    down(cy, 12, start)
    arrive(8 + cy)
    up(cy, 9, start)
    arrive(12 + cx)
    down(cx, 11, start)
    arrive(8 + cd)
    up(cd, 10, start)
    arrive(12 + cd)
    down(cd, 13, start)

    @pl.when(p == groups - 1)
    def _():
        for c in range(4):
            kv[16 + c] = kv[11 - c]

    for c in (b, *peers):

        @pl.when(has_below)
        def _():
            arrive(4 + c)

        up_again(c, start)

        @pl.when(has_above)
        def _():
            arrive(16 + c)

        down_again(c, start)

    @pl.when(p == groups - 1)
    def _():
        for c in range(3):
            kv[20 + c] = kv[7 - c]

    def far_arrive():
        for c in range(GROUP):

            @pl.when((p >= 2) & (c > b))
            def _():
                arrive(c)

            @pl.when((p < groups - 1) & (c < b))
            def _():
                arrive(20 + c)

    scale = math.log2(math.e) / math.sqrt(HEAD_WIDTH)
    q_copy.wait()
    bounds = [jnp.int32(0)]
    for n in range(docs.shape[0]):
        bounds.append(bounds[-1] + docs[n])

    def attend(x, far, state):
        stretch = x * last + (1 - 2 * x) * i
        base = pl.multiple_of(x * half, half)
        here = stretch * half + lax.broadcasted_iota(jnp.int32, (half, 1), 0)
        start = jnp.zeros((half, 1), jnp.int32)
        for end in bounds[1:]:
            start = jnp.maximum(start, jnp.where(end <= here, end, 0))
        first = b + 5 - 4 * far + x * (7 + 8 * far)
        part = kv[pl.ds(first, CHUNK)]
        k = part[:, 0].reshape(CHUNK * half, HEAD_WIDTH)
        v = part[:, 1].reshape(CHUNK * half, HEAD_WIDTH)
        column = lax.broadcasted_iota(jnp.int32, (1, CHUNK * half), 1)
        block = column // half
        order = (1 - x) * (block - CHUNK + 1) - x * block - CHUNK * far
        there = (stretch + order) * half + column - half * block
        bias = jnp.where((there >= start) & (there <= here), 0.0, NEG_FILL)
        made = []
        for h in range(heads):
            lanes = slice(h * HEAD_WIDTH, (h + 1) * HEAD_WIDTH)
            score = (
                lax.dot_general(
                    q[pl.ds(base, half), lanes],
                    k,
                    (((1,), (1,)), ((), ())),
                    preferred_element_type=jnp.float32,
                )
                + bias
            )
            top = jnp.max(score, axis=1, keepdims=True)
            if far:
                top = jnp.maximum(top, state[h][0])
            weight = jnp.exp2((score - top) * scale)
            total = jnp.sum(weight, axis=1, keepdims=True)
            out = jnp.dot(weight.astype(jnp.bfloat16), v, preferred_element_type=jnp.float32)
            if far:
                factor = jnp.exp2((state[h][0] - top) * scale)
                total = total + state[h][1] * factor
                out = out + state[h][2] * factor
                att[pl.ds(base, half), lanes] = (out / total).astype(att.dtype)
            made.append((top, total, out))
        return made

    def project(part, t):
        return jnp.dot(
            att[pl.ds(pl.multiple_of(part * out_rows, out_rows), out_rows), :],
            w[:, t * TILE : (t + 1) * TILE],
            preferred_element_type=jnp.float32,
        )

    def hand_over(j, t):
        return pltpu.make_async_remote_copy(
            src_ref=sbuf.at[j - 1, t],
            dst_ref=rbuf.at[j - 1, t],
            send_sem=rs_send.at[j - 1, t],
            recv_sem=rs_recv.at[j - 1, t],
            device_id={"kvh": lax.rem(g + j, n_kvh)},
            device_id_type=pl.DeviceIdType.MESH,
        )

    def give():
        for j in range(1, n_kvh):
            for t in range(tiles):
                sbuf[j - 1, t] = project(lax.rem(g + j, n_kvh), t).astype(sbuf.dtype)
                hand_over(j, t).start()

    split = n_kvh == 2
    sides = (1 - g, g) if split else (0, 1)
    near = [attend(x, 0, None) for x in sides]
    far_arrive()
    attend(sides[0], 1, near[0])
    if split:
        w_copy.wait()
        give()
        attend(sides[1], 1, near[1])
    else:
        attend(sides[1], 1, near[1])
        w_copy.wait()
        give()
    for t in range(tiles):
        total = project(g, t)
        for j in range(1, n_kvh):
            hand_over(j, t).wait_recv()
            total = total + rbuf[j - 1, t].astype(jnp.float32)
        o_ref[:, t * TILE : (t + 1) * TILE] = total.astype(o_ref.dtype)

    def sent(copy):
        copy.wait_send()

    up(b, 6, sent)
    down(b, 7, sent)
    give_own(0, sent)
    give_own(1, sent)
    pass_on(sent)
    for k, c in enumerate(peers):
        up(c, 8 + k, sent)
        down(c, 11 + k, sent)
    for c in (b, *peers):
        up_again(c, sent)
        down_again(c, sent)
    for j in range(1, n_kvh):
        for t in range(tiles):
            hand_over(j, t).wait_send()


def local(n_ctx, n_kvh, doc_lengths, queries, keys, values, o_weight):
    rows, width = queries.shape
    half = rows // 2
    columns = o_weight.shape[1]
    out_rows = rows // n_kvh
    tiles = columns // TILE
    dtype = queries.dtype
    any_spec = pl.BlockSpec(memory_space=pl.ANY)
    return pl.pallas_call(
        functools.partial(kernel, n_ctx, n_kvh),
        out_shape=jax.ShapeDtypeStruct((out_rows, columns), dtype),
        in_specs=[pl.BlockSpec(memory_space=pltpu.SMEM)] + [any_spec] * 4,
        out_specs=pl.BlockSpec(memory_space=pltpu.VMEM),
        scratch_shapes=[
            pltpu.VMEM((6 * GROUP, 2, half, HEAD_WIDTH), dtype),
            pltpu.VMEM((rows, width), dtype),
            pltpu.VMEM(o_weight.shape, dtype),
            pltpu.VMEM((rows, width), dtype),
            pltpu.VMEM((n_kvh - 1, tiles, out_rows, TILE), dtype),
            pltpu.VMEM((n_kvh - 1, tiles, out_rows, TILE), dtype),
            pltpu.SemaphoreType.DMA((6,)),
            pltpu.SemaphoreType.DMA((22,)),
            pltpu.SemaphoreType.DMA((6 * GROUP,)),
            pltpu.SemaphoreType.DMA((n_kvh - 1, tiles)),
            pltpu.SemaphoreType.DMA((n_kvh - 1, tiles)),
        ],
        compiler_params=pltpu.CompilerParams(
            collective_id=0, has_side_effects=True, vmem_limit_bytes=60 * 2**20
        ),
    )(doc_lengths, queries, keys, values, o_weight)

def solution(mesh):
    in_specs = (P(), P("ctx", "kvh"), P("ctx", "kvh"), P("ctx", "kvh"), P("kvh", None))
    out_specs = P(("ctx", "kvh"), None)
    return jax.shard_map(
        functools.partial(local, mesh.shape["ctx"], mesh.shape["kvh"]),
        mesh=mesh,
        in_specs=in_specs,
        out_specs=out_specs,
        check_vma=False,
    )
```
